256 devices in a mesh: row: 32 (over z, x), col: 8 (over y, core).
Axes of the slice: x: 4, y: 4, z: 8, core: 2. Of those that a mesh axis runs over, the one named last changes fastest.
Arguments:
- activations: bfloat16 [4096, 26624], P('col', 'row'), may hold values from -6 to 6
- d_out: bfloat16 [4096, 8192], P('row', 'col'), may hold values from -60 to 60
- levels: bfloat16 [26624, 8192], P('row', 'col'), may hold values from -6 to 6
- scales: float32 [8192], P('col'), may hold values from 0.002 to 0.02
- clip_mask: int32 [26624, 8192], P('row', 'col'), may hold values 0 or 1
Outputs:
- d_in: float32 [4096, 26624], P('col', 'row')
- d_levels: float32 [26624, 8192], P('row', 'col')
The draws below stay inside these ranges and needn't reach their ends.
All inputs are finite; a program needn't handle non-finite values. Where the reference program divides by a largest or mean magnitude, that divisor is 1e-20 or more. No bound on the sum of `clip_mask` on one device may be relied on, other than what follows from the above.
Results may differ from the reference program's by a relative error of at most 0.004.
Values may be sent and summed in bfloat16 or wider, within the bound.
A program may use at most 128 MiB of HBM per device.

```python
import math
import jax
import jax.numpy as jnp
from jax import lax

K = 26624
PANEL = 8192
TOKENS = 4096


def draw_d_out(key, part):
    key = jax.random.fold_in(key, 11)
    key_base, key_cols = jax.random.split(key, 2)
    positions = jnp.arange(TOKENS, dtype=jnp.float32)[:, None]
    rising = 3.0 ** (positions / TOKENS)
    columns = 10.0 ** jax.random.uniform(key_cols, (1, PANEL), dtype=jnp.float32)
    base = jnp.clip(jax.random.normal(key_base, (TOKENS, PANEL), dtype=jnp.float32), -6.0, 6.0)
    values = base * rising * columns / 3.0
    return values.astype(jnp.bfloat16)


def touch_ends(entries, stream_key, smallest, largest):
    spot = [jax.random.randint(jax.random.fold_in(stream_key, axis), (), 0, length) for axis, length in enumerate(entries.shape)]
    main_axis = entries.shape.index(max(entries.shape))
    next_to = spot[:main_axis] + [(spot[main_axis] + 1) % entries.shape[main_axis]] + spot[main_axis + 1:]
    return entries.at[tuple(spot)].set(smallest).at[tuple(next_to)].set(largest)


def block_scale(key, extent, pieces, low, largest):
    factor_of, own = 1.0, jax.random.fold_in(key, 6)
    for axis_at, shards_of in pieces:
        draws = jnp.exp(jax.random.uniform(jax.random.fold_in(own, axis_at), (shards_of,), jnp.float32, low / len(pieces), largest / len(pieces)))
        factor_of = factor_of * jnp.repeat(draws, extent[axis_at] // shards_of).reshape([-1 if axis == axis_at else 1 for axis in range(len(extent))])
    return factor_of


def bell_draw(own_key, extent, scale, limit, cuts=(), kind=jnp.bfloat16):
    drawn = jax.random.normal(own_key, extent, jnp.float32) * scale
    if len(cuts) > 0:
        drawn = block_scale(own_key, extent, cuts, -0.22, 0.18) * drawn
    return jnp.clip(drawn, min=-limit, max=limit).astype(kind)


def setup_inputs(seed: int = 0) -> dict:
    splits = jax.random.split(jax.random.key(seed), 6)
    activations = bell_draw(splits[0], (TOKENS, K), 1.0, 6.0, ((0, 8), (1, 32)))
    d_out = draw_d_out(jax.random.fold_in(splits[5], 71), 0)
    levels = bell_draw(splits[2], (K, PANEL), 1.0, 6.0, ((0, 32), (1, 8)))
    scales = jnp.clip(jnp.exp(math.log(0.02) - 2.30258502 * jax.random.uniform(splits[3], (PANEL,), jnp.float32) ** block_scale(splits[3], (PANEL,), ((0, 8),), -0.2, 0.2)), 0.002, 0.02)
    clip_mask = touch_ends((jax.random.randint(splits[4], (K, PANEL), 0, 8) < 7).astype(jnp.int32), jax.random.fold_in(splits[4], 1), 0, 1)
    return {"activations": activations, "d_out": d_out, "levels": levels, "scales": scales, "clip_mask": clip_mask}


peak_level = 4.0
eps = 1e-6


def reference(activations, d_out, levels, scales, clip_mask):
    raw = d_out.astype(jnp.float32)
    amax = jnp.max(jnp.abs(raw))
    grad_scale = peak_level / (amax + eps)
    quant = (raw * grad_scale).astype(jnp.bfloat16)
    dequant = (levels.astype(jnp.float32) * scales[None, :]).astype(jnp.bfloat16)
    d_in = lax.dot_general(quant, dequant, (((1,), (1,)), ((), ())), preferred_element_type=jnp.float32)
    product = lax.dot_general(activations, quant, (((0,), (0,)), ((), ())), preferred_element_type=jnp.float32)
    d_levels = clip_mask.astype(jnp.float32) * scales[None, :] * product
    return d_in, d_levels
```

```python
import jax
import jax.numpy as jnp
from jax import lax
from jax.experimental import pallas as pl
from jax.experimental.pallas import tpu as pltpu
from jax.sharding import PartitionSpec as P

peak_level = 4.0
eps = 1e-06

MESH = pl.DeviceIdType.MESH
NT = (((1,), (1,)), ((), ()))
NN = (((1,), (0,)), ((), ()))
F32 = jnp.float32
BF16 = jnp.bfloat16

K = 832
T = 512
C = 1024
XF = 48
HALF = K // 2
LO = pl.ds(0, HALF)
HI = pl.ds(HALF, HALF)
CH = 208
N_EV = 96

OFFS = (0, 1, 7, 2, 6, 3, 5, 4)


def up(h):
    return 2 * h - 1


def down(h):
    return 7 if h == 4 else 2 * h


def kernel(act, dout, levels, scales, mask, din_out, dlev_out,
           D, A, W, acc, Cs, Ssend, Srecv, Y, rel, fin, lev_v, mask_v, mx, Mx,
           ss, rs, ls):
    row, col = lax.axis_index("row"), lax.axis_index("col")
    z, x = row // 4, row % 4
    y, k = col // 2, col % 2

    def dev(dz=0, dx=0, dy=0, dk=0):
        return (((z + dz) % 8) * 4 + (x + dx) % 4, ((y + dy) % 4) * 2 + (k + dk) % 2)

    zp, zm, xp, xm, xx = dev(dz=1), dev(dz=7), dev(dx=1), dev(dx=3), dev(dx=2)
    yp, ym, yy, kk = dev(dy=1), dev(dy=3), dev(dy=2), dev(dk=1)

    ev = {}

    def plan(name, src, dst, to):
        ev[name] = (len(ev), src, dst, to)

    def copy_of(name):
        i, src, dst, to = ev[name]
        return pltpu.make_async_remote_copy(
            src_ref=src, dst_ref=dst, send_sem=ss.at[i], recv_sem=rs.at[i],
            device_id=to, device_id_type=MESH)

    def send(name, *what):
        if what:
            plan(name, *what)
        copy_of(name).start()

    def got(*names):
        for n in names:
            copy_of(n).wait_recv()

    plan("relL", Y.at[2, LO], rel.at[0], yp)
    plan("relU", Y.at[2, HI], rel.at[1], ym)
    plan("fmU", Y.at[0, HI], fin.at[0, HI], yp)
    plan("fmL", Y.at[0, LO], fin.at[0, LO], yp)
    plan("fpU", Y.at[1, HI], fin.at[1, HI], ym)
    plan("fpL", Y.at[1, LO], fin.at[1, LO], ym)
    for s in range(8):
        d = ((z + OFFS[s]) % 8 // 2 + 4 - y) % 4
        plan(f"sib{s}", Ssend.at[d], Srecv.at[d], kk)

    own = 2 * y + k
    l_d = pltpu.make_async_copy(dout, D.at[0, x], ls.at[0])
    l_a = pltpu.make_async_copy(act, A.at[own], ls.at[1])
    l_w = pltpu.make_async_copy(levels, lev_v, ls.at[2])
    l_m = pltpu.make_async_copy(mask, mask_v, ls.at[3])

    barrier = pltpu.get_barrier_semaphore()
    peers = (zp, zm, xp, xm, xx, yp, ym, yy, kk)
    for p in peers:
        pl.semaphore_signal(barrier, inc=1, device_id=p, device_id_type=MESH)
    l_d.start()
    l_w.start()
    l_a.start()
    pl.semaphore_wait(barrier, len(peers))

    a_rows, b_rows = pl.ds(0, XF), pl.ds(XF, 128 - XF)
    b_lo, b_hi = pl.ds(XF, 48), pl.ds(XF + 48, 80 - 48)

    send("xA+", dout.at[a_rows], D.at[0, x, a_rows], xp)
    send("xA-", dout.at[a_rows], D.at[0, x, a_rows], xm)
    send("zB+1", dout.at[b_rows], D.at[down(1), x, b_rows], zp)
    send("zB-1", dout.at[b_rows], D.at[up(1), x, b_rows], zm)
    send("xA2", dout.at[a_rows], D.at[0, x, a_rows], xx)
    send("aL+", act.at[LO], A.at[own, LO], yp)
    send("aU-", act.at[HI], A.at[own, HI], ym)
    send("xB+0", dout.at[b_rows], D.at[0, x, b_rows], xp)
    send("xB-0", dout.at[b_rows], D.at[0, x, b_rows], xm)
    send("aU+", act.at[HI], A.at[own, HI], yp)
    send("aL-", act.at[LO], A.at[own, LO], ym)
    send("ak0", act, A.at[own], kk)
    l_m.start()

    l_w.wait()

    def deq(i, _):
        r = pl.multiple_of(i * CH, 16)
        W[pl.ds(r, CH), :] = (lev_v[pl.ds(r, CH), :].astype(F32) * scales[...]).astype(BF16)
        return 0

    lax.fori_loop(0, K // CH, deq, 0)
    mx[...] = jnp.zeros_like(mx)
    l_d.wait()

    def fwd_z(h):
        got(f"zB+{h}", f"zB-{h}")
        if h < 3:
            send(f"zB+{h+1}", D.at[down(h), x, b_rows], D.at[down(h + 1), x, b_rows], zp)
            send(f"zB-{h+1}", D.at[up(h), x, b_rows], D.at[up(h + 1), x, b_rows], zm)
        if h == 3:
            send("zB+4", D.at[down(3), x, b_lo], D.at[7, x, b_lo], zp)
            send("zB-4", D.at[up(3), x, b_hi], D.at[7, x, b_hi], zm)
        if h < 4:
            pair = D.at[pl.ds(2 * h - 1, 2), x, b_rows]
        else:
            pair = D.at[7, x, b_rows]
        send(f"xB+{h}", pair, pair, xp)
        send(f"xB-{h}", pair, pair, xm)

    def fwd_a(h):
        if h == 0:
            got("xA+", "xA-", "xA2")
        elif h < 4:
            got(f"zA0+{h}", f"zA0-{h}", f"zA1+{h}", f"zA1-{h}")
        else:
            got("zA0+4", "zA1-4")
            return
        lo, hi = (0, 0) if h == 0 else (down(h), up(h))
        for j in range(2):
            xs = pl.ds(2 * j, 2)
            if h < 3 or j == 0:
                send(f"zA{j}+{h+1}", D.at[lo, xs, a_rows], D.at[down(h + 1), xs, a_rows], zp)
            if h < 3 or j == 1:
                send(f"zA{j}-{h+1}", D.at[hi, xs, a_rows], D.at[up(h + 1) if h < 3 else 7, xs, a_rows], zm)

    xl, xr = (x + 3) % 4, (x + 1) % 4

    def relay_x(h):
        got(f"xB+{h}", f"xB-{h}")
        if h in (0, 4):
            s = 0 if h == 0 else 7
            r0, r1 = D.at[s, xl, b_lo], D.at[s, xr, b_hi]
        else:
            r0, r1 = D.at[up(h), xl, b_rows], D.at[down(h), xr, b_rows]
        send(f"xr+{h}", r0, r0, xp)
        send(f"xr-{h}", r1, r1, xm)

    def relayed_x(h):
        got(f"xr+{h}", f"xr-{h}")

    def where(s):
        b = (z + OFFS[s]) % 8
        return b, b % 2 == k, (b // 2 + 4 - y) % 4

    def mm1(s):
        b, mine, d = where(s)

        def part():
            return lax.dot_general(W[...], D[s].reshape(T, C), NT, preferred_element_type=F32)

        @pl.when(mine)
        def _():
            Cs[d] = part()

        @pl.when(jnp.logical_not(mine))
        def _():
            Ssend[d] = part().astype(BF16)
            send(f"sib{s}")

        def big(i, m):
            r = pl.multiple_of(i * 16, 16)
            return jnp.maximum(m, jnp.abs(Dm[s, pl.ds(r, 16), :]))

        Dm = D.reshape(8, T, C)
        mx[...] = lax.fori_loop(0, T // 16, big, mx[...], unroll=4)

    def rows_of(lo, n, fn):
        def body(i, _):
            fn(pl.ds(pl.multiple_of(lo + i * CH, 16), CH))
            return 0
        lax.fori_loop(0, n // CH, body, 0)

    def pair_sum(d, r):
        return Cs[d, r, :] + Srecv[d, r, :].astype(F32)

    def stage2(s):
        b, mine, d = where(s)

        @pl.when(mine)
        def _():
            got(f"sib{s}")

            @pl.when(d == 2)
            def _():
                def f(r):
                    Y[2, r, :] = pair_sum(2, r).astype(BF16)
                rows_of(0, K, f)
                send("relL")
                send("relU")

            @pl.when(d == 1)
            def _():
                def f(r):
                    Y[0, r, :] = pair_sum(1, r).astype(BF16)
                rows_of(HALF, HALF, f)
                send("fmU")

            @pl.when(d == 3)
            def _():
                def f(r):
                    Y[1, r, :] = pair_sum(3, r).astype(BF16)
                rows_of(0, HALF, f)
                send("fpL")

    def stage3(s):
        b, mine, d = where(s)

        @pl.when(jnp.logical_and(mine, d == 1))
        def _():
            got("relL")

            def f(r):
                Y[0, r, :] = (pair_sum(1, r) + rel[0, r, :].astype(F32)).astype(BF16)
            rows_of(0, HALF, f)
            send("fmL")

        @pl.when(jnp.logical_and(mine, d == 3))
        def _():
            got("relU")

            def f(i, _):
                r = pl.ds(pl.multiple_of(HALF + i * CH, 16), CH)
                q = pl.ds(pl.multiple_of(i * CH, 16), CH)
                Y[1, r, :] = (pair_sum(3, r) + rel[1, q, :].astype(F32)).astype(BF16)
                return 0
            lax.fori_loop(0, HALF // CH, f, 0)
            send("fpU")

    def mm2(s):
        b, _, _ = where(s)

        def f(j, _):
            c = pl.ds(pl.multiple_of(j * 256, 256), 256)
            v = lax.dot_general(A[b], D.at[s][:, :, c].reshape(T, 256), NN, preferred_element_type=F32)
            if s == 0:
                acc[:, c] = v
            else:
                acc[:, c] += v
            return 0
        lax.fori_loop(0, C // 256, f, 0)

    def act_relay():
        got("aL+", "aU-")
        bl, br = (own + 6) % 8, (own + 2) % 8
        send("aR+", A.at[bl, LO], A.at[bl, LO], yp)
        send("aR-", A.at[br, HI], A.at[br, HI], ym)

    def act_pass():
        got("aU+", "aL-")
        bl, br = (own + 6) % 8, (own + 2) % 8
        send("ak1", A.at[bl], A.at[bl], kk)
        send("ak2", A.at[br], A.at[br], kk)

    def act_far():
        got("aR+", "aR-")
        bb = (own + 4) % 8
        send("ak3", A.at[bb], A.at[bb], kk)

    fwd_a(0)
    fwd_z(1)
    relay_x(0)
    act_relay()
    relayed_x(0)
    mm1(0)
    fwd_z(2)
    fwd_a(1)
    relay_x(1)
    stage2(0)
    act_pass()
    fwd_z(3)
    relayed_x(1)
    mm1(1)
    mm1(2)
    fwd_a(2)
    relay_x(2)
    stage2(1)
    stage2(2)
    fwd_z(4)
    act_far()
    relayed_x(2)
    mm1(3)
    mm1(4)
    fwd_a(3)
    relay_x(3)
    l_a.wait()
    got("ak0", "ak1", "ak2", "ak3")
    mm2(0)
    stage2(3)
    stage2(4)
    mm2(1)
    stage3(0)
    stage3(1)
    stage3(2)
    relayed_x(3)
    mm1(5)
    mm1(6)
    relay_x(4)
    mm2(2)
    stage2(5)
    stage2(6)
    stage3(3)
    stage3(4)
    fwd_a(4)
    relayed_x(4)
    mm1(7)
    Mx[0] = jnp.broadcast_to(jnp.max(mx[...].astype(F32)), (8, 128))
    send("mk", Mx.at[0], Mx.at[1], kk)
    mm2(3)
    stage2(7)
    got("mk")
    Mx[2] = jnp.maximum(Mx[0], Mx[1])
    send("m1", Mx.at[2], Mx.at[3], yp)
    send("m2", Mx.at[2], Mx.at[4], ym)
    send("m3", Mx.at[2], Mx.at[5], yy)
    mm2(4)
    stage3(5)
    stage3(6)
    mm2(5)
    mm2(6)
    stage3(7)
    mm2(7)
    got("m1", "m2", "m3")
    amax = jnp.maximum(jnp.maximum(Mx[2], Mx[3]), jnp.maximum(Mx[4], Mx[5]))
    gain = (peak_level / (amax + eps))[0:1, 0:1]
    factor = gain * scales[...]
    l_m.wait()
    outs = []
    for i in range(K // CH):
        r = pl.ds(i * CH, CH)
        acc[r, :] = mask_v[r, :].astype(F32) * factor * acc[r, :]
        c = pltpu.make_async_copy(acc.at[r], dlev_out.at[r], ls.at[4 + i])
        c.start()
        outs.append(c)
    got("fmU", "fmL", "fpL", "fpU")
    for i in range(K // CH):
        r = pl.ds(i * CH, CH)
        total = pair_sum(0, r) + fin[0, r, :].astype(F32) + fin[1, r, :].astype(F32)
        Cs[0, r, :] = total * gain
        c = pltpu.make_async_copy(Cs.at[0, r], din_out.at[r], ls.at[8 + i])
        c.start()
        outs.append(c)
    for c in outs:
        c.wait()
    some = {f"sib{s}" for s in range(8)}
    for n in ev:
        if n not in some:
            copy_of(n).wait_send()
    for s in range(8):
        b, mine, d = where(s)

        @pl.when(jnp.logical_not(mine))
        def _():
            copy_of(f"sib{s}").wait_send()


def on_device(activations, d_out, levels, scales, clip_mask):
    any_ = pl.BlockSpec(memory_space=pl.ANY)
    vm = pltpu.VMEM
    d_in_t, d_levels = pl.pallas_call(
        kernel,
        out_shape=(jax.ShapeDtypeStruct((K, T), F32), jax.ShapeDtypeStruct((K, C), F32)),
        in_specs=[any_, any_, any_, pl.BlockSpec(memory_space=vm), any_],
        out_specs=(any_, any_),
        scratch_shapes=[
            vm((8, 4, 128, C), BF16),
            vm((8, K, T), BF16),
            vm((K, C), BF16),
            vm((K, C), F32),
            vm((4, K, T), F32),
            vm((4, K, T), BF16),
            vm((4, K, T), BF16),
            vm((3, K, T), BF16),
            vm((2, HALF, T), BF16),
            vm((2, K, T), BF16),
            vm((K, C), BF16),
            vm((K, C), jnp.int32),
            vm((16, C), BF16),
            vm((6, 8, 128), F32),
            pltpu.SemaphoreType.DMA((N_EV,)),
            pltpu.SemaphoreType.DMA((N_EV,)),
            pltpu.SemaphoreType.DMA((12,)),
        ],
        compiler_params=pltpu.CompilerParams(
            collective_id=0, has_side_effects=True, vmem_limit_bytes=60 * 2**20),
        cost_estimate=pl.CostEstimate(flops=4 * 4096 * K * C, bytes_accessed=12 * 2**20, transcendentals=0),
        name="fused",
    )(activations.T, d_out, levels, scales.reshape(1, C), clip_mask)
    return d_in_t.T, d_levels


def solution(mesh):
    placed = (P("col", "row"), P("row", "col"), P("row", "col"), P("col"), P("row", "col"))
    return jax.shard_map(
        on_device,
        mesh=mesh,
        in_specs=placed,
        out_specs=(P("col", "row"), P("row", "col")),
        check_vma=False,
    )
```

```python
import jax
import jax.numpy as jnp
from jax import lax
from jax.experimental import pallas as pl
from jax.experimental.pallas import tpu as pltpu
from jax.sharding import PartitionSpec as P

peak_level = 4.0
eps = 1e-06

MESH = pl.DeviceIdType.MESH
NT = (((1,), (1,)), ((), ()))
NN = (((1,), (0,)), ((), ()))
F32 = jnp.float32
BF16 = jnp.bfloat16

K = 832
T = 512
N = 256
C = 1024
XF = 48
HALF = K // 2
LO = pl.ds(0, HALF)
HI = pl.ds(HALF, HALF)
CH = 208
N_EV = 96

OFFS = (0, 1, 7, 2, 6, 3, 5, 4)


def up(h):
    return 2 * h - 1


def down(h):
    return 7 if h == 4 else 2 * h


def kernel(act, dout, levels, scales, mask, din, acc,
           D, A, W, Cs, Ssend, Srecv, Y, rel, fin, lev_v, mask_v, mx, Mx,
           ss, rs, ls):
    row, col = lax.axis_index("row"), lax.axis_index("col")
    z, x = row // 4, row % 4
    y, k = col // 2, col % 2

    def dev(dz=0, dx=0, dy=0, dk=0):
        return (((z + dz) % 8) * 4 + (x + dx) % 4, ((y + dy) % 4) * 2 + (k + dk) % 2)

    zp, zm, xp, xm = dev(dz=1), dev(dz=7), dev(dx=1), dev(dx=3)
    yp, ym, yy, kk = dev(dy=1), dev(dy=3), dev(dy=2), dev(dk=1)

    ev = {}

    def plan(name, src, dst, to):
        ev[name] = (len(ev), src, dst, to)

    def copy_of(name):
        i, src, dst, to = ev[name]
        return pltpu.make_async_remote_copy(
            src_ref=src, dst_ref=dst, send_sem=ss.at[i], recv_sem=rs.at[i],
            device_id=to, device_id_type=MESH)

    def send(name, *what):
        if what:
            plan(name, *what)
        copy_of(name).start()

    def got(*names):
        for n in names:
            copy_of(n).wait_recv()

    for p in range(2):
        plan(f"relL{p}", Y.at[2, p, LO], rel.at[0, p], yp)
        plan(f"relU{p}", Y.at[2, p, HI], rel.at[1, p], ym)
        plan(f"fmU{p}", Y.at[0, p, HI], fin.at[0, p, HI], yp)
        plan(f"fmL{p}", Y.at[0, p, LO], fin.at[0, p, LO], yp)
        plan(f"fpU{p}", Y.at[1, p, HI], fin.at[1, p, HI], ym)
        plan(f"fpL{p}", Y.at[1, p, LO], fin.at[1, p, LO], ym)
        for s in range(8):
            d = ((z + OFFS[s]) % 8 // 2 + 4 - y) % 4
            plan(f"sib{s}{p}", Ssend.at[d, p], Srecv.at[d, p], kk)
    xs = (x // 2 * 2, 2 - x // 2 * 2)

    own = 2 * y + k
    l_d = pltpu.make_async_copy(dout, D.at[0, x], ls.at[0])
    l_a = pltpu.make_async_copy(act, A.at[own], ls.at[1])
    l_w = pltpu.make_async_copy(levels, lev_v, ls.at[2])
    l_m = pltpu.make_async_copy(mask, mask_v, ls.at[3])

    barrier = pltpu.get_barrier_semaphore()
    peers = (zp, zm, xp, xm, yp, ym, yy, kk)
    for p in peers:
        pl.semaphore_signal(barrier, inc=1, device_id=p, device_id_type=MESH)
    l_d.start()
    l_w.start()
    l_a.start()
    pl.semaphore_wait(barrier, len(peers))

    a_rows, b_rows = pl.ds(0, XF), pl.ds(XF, 128 - XF)
    b_lo, b_hi = pl.ds(XF, 48), pl.ds(XF + 48, 80 - 48)

    send("xA+", dout.at[a_rows], D.at[0, x, a_rows], xp)
    send("xA-", dout.at[a_rows], D.at[0, x, a_rows], xm)
    send("zB+1", dout.at[b_rows], D.at[down(1), x, b_rows], zp)
    send("zB-1", dout.at[b_rows], D.at[up(1), x, b_rows], zm)
    send("aL+", act.at[LO], A.at[own, LO], yp)
    send("aU-", act.at[HI], A.at[own, HI], ym)
    send("xB+0", dout.at[b_rows], D.at[0, x, b_rows], xp)
    send("xB-0", dout.at[b_rows], D.at[0, x, b_rows], xm)
    send("aU+", act.at[HI], A.at[own, HI], yp)
    send("aL-", act.at[LO], A.at[own, LO], ym)
    send("ak0", act, A.at[own], kk)
    l_m.start()

    l_w.wait()

    def deq(i, _):
        r = pl.multiple_of(i * CH, 16)
        W[pl.ds(r, CH), :] = (lev_v[pl.ds(r, CH), :].astype(F32) * scales[...]).astype(BF16)
        return 0

    lax.fori_loop(0, K // CH, deq, 0)
    mx[...] = jnp.zeros_like(mx)
    l_d.wait()

    def fwd_z(h):
        got(f"zB+{h}", f"zB-{h}")
        if h < 3:
            send(f"zB+{h+1}", D.at[down(h), x, b_rows], D.at[down(h + 1), x, b_rows], zp)
            send(f"zB-{h+1}", D.at[up(h), x, b_rows], D.at[up(h + 1), x, b_rows], zm)
        if h == 3:
            send("zB+4", D.at[down(3), x, b_lo], D.at[7, x, b_lo], zp)
            send("zB-4", D.at[up(3), x, b_hi], D.at[7, x, b_hi], zm)

    def spread_x(h):
        pair = D.at[pl.ds(2 * h - 1, 2), x, b_rows] if h < 4 else D.at[7, x, b_rows]
        send(f"xB+{h}", pair, pair, xp)
        send(f"xB-{h}", pair, pair, xm)

    def fwd_a(h, p):
        if h == 0:
            if p == 0:
                got("xA+", "xA-")
            else:
                got("xR+", "xR-")
        elif h < 3:
            got(f"zA{p}+{h}", f"zA{p}-{h}")
        elif h == 3:
            got("zA0+3" if p == 0 else "zA1-3")
        else:
            got("zA0+4" if p == 0 else "zA1-4")
        if h == 4:
            return
        lo, hi = (0, 0) if h == 0 else (down(h), up(h))
        q = pl.ds(xs[p], 2)
        if h < 3 or p == 0:
            send(f"zA{p}+{h+1}", D.at[lo, q, a_rows], D.at[down(h + 1), q, a_rows], zp)
        if h < 3 or p == 1:
            send(f"zA{p}-{h+1}", D.at[hi, q, a_rows], D.at[up(h + 1) if h < 3 else 7, q, a_rows], zm)

    xl, xr = (x + 3) % 4, (x + 1) % 4

    def rest_a(p):
        got("zA0-3" if p == 0 else "zA1+3")

    def relay_a():
        r0, r1 = D.at[0, xl, pl.ds(0, 32)], D.at[0, xr, pl.ds(32, 16)]
        send("xR+", r0, r0, xp)
        send("xR-", r1, r1, xm)

    def relay_x(h):
        got(f"xB+{h}", f"xB-{h}")
        if h in (0, 4):
            s = 0 if h == 0 else 7
            r0, r1 = D.at[s, xl, b_lo], D.at[s, xr, b_hi]
        else:
            r0, r1 = D.at[up(h), xl, b_rows], D.at[down(h), xr, b_rows]
        send(f"xr+{h}", r0, r0, xp)
        send(f"xr-{h}", r1, r1, xm)

    def relayed_x(h):
        got(f"xr+{h}", f"xr-{h}")

    def where(s):
        b = (z + OFFS[s]) % 8
        return b, b % 2 == k, (b // 2 + 4 - y) % 4

    def mm1(s, p):
        b, mine, d = where(s)
        q = pl.ds(xs[p], 2)

        def part():
            return lax.dot_general(W[...], D[s, q].reshape(N, C), NT, preferred_element_type=F32)

        @pl.when(mine)
        def _():
            Cs[d, p] = part()

        @pl.when(jnp.logical_not(mine))
        def _():
            Ssend[d, p] = part().astype(BF16)
            send(f"sib{s}{p}")

        for j in range(2):
            def big(i, m):
                r = pl.multiple_of(i * 16, 16)
                return jnp.maximum(m, jnp.abs(D[s, xs[p] + j, pl.ds(r, 16), :]))

            mx[...] = lax.fori_loop(0, 8, big, mx[...], unroll=4)

    def rows_of(lo, n, fn):
        def body(i, _):
            fn(pl.ds(pl.multiple_of(lo + i * CH, 16), CH))
            return 0
        lax.fori_loop(0, n // CH, body, 0)

    def pair_sum(d, p, r):
        return Cs[d, p, r, :] + Srecv[d, p, r, :].astype(F32)

    def stage2(s, p):
        b, mine, d = where(s)

        @pl.when(mine)
        def _():
            got(f"sib{s}{p}")

            @pl.when(d == 2)
            def _():
                def f(r):
                    Y[2, p, r, :] = pair_sum(2, p, r).astype(BF16)
                rows_of(0, K, f)
                send(f"relL{p}")
                send(f"relU{p}")

            @pl.when(d == 1)
            def _():
                def f(r):
                    Y[0, p, r, :] = pair_sum(1, p, r).astype(BF16)
                rows_of(HALF, HALF, f)
                send(f"fmU{p}")

            @pl.when(d == 3)
            def _():
                def f(r):
                    Y[1, p, r, :] = pair_sum(3, p, r).astype(BF16)
                rows_of(0, HALF, f)
                send(f"fpL{p}")

    def stage3(s, p):
        b, mine, d = where(s)

        @pl.when(jnp.logical_and(mine, d == 1))
        def _():
            got(f"relL{p}")

            def f(r):
                Y[0, p, r, :] = (pair_sum(1, p, r) + rel[0, p, r, :].astype(F32)).astype(BF16)
            rows_of(0, HALF, f)
            send(f"fmL{p}")

        @pl.when(jnp.logical_and(mine, d == 3))
        def _():
            got(f"relU{p}")

            def f(i, _):
                r = pl.ds(pl.multiple_of(HALF + i * CH, 16), CH)
                q = pl.ds(pl.multiple_of(i * CH, 16), CH)
                Y[1, p, r, :] = (pair_sum(3, p, r) + rel[1, p, q, :].astype(F32)).astype(BF16)
                return 0
            lax.fori_loop(0, HALF // CH, f, 0)
            send(f"fpU{p}")

    def mm2(s):
        b, _, _ = where(s)

        def f(j, _):
            c = pl.ds(pl.multiple_of(j * 256, 256), 256)
            v = lax.dot_general(A[b], D.at[s][:, :, c].reshape(T, 256), NN, preferred_element_type=F32)
            if s == 0:
                acc[:, c] = v
            else:
                acc[:, c] += v
            return 0
        lax.fori_loop(0, C // 256, f, 0)

    def act_relay():
        got("aL+", "aU-")
        bl, br = (own + 6) % 8, (own + 2) % 8
        send("aR+", A.at[bl, LO], A.at[bl, LO], yp)
        send("aR-", A.at[br, HI], A.at[br, HI], ym)

    def act_pass():
        got("aU+", "aL-")
        bl, br = (own + 6) % 8, (own + 2) % 8
        send("ak1", A.at[bl], A.at[bl], kk)
        send("ak2", A.at[br], A.at[br], kk)

    def act_far():
        got("aR+", "aR-")
        bb = (own + 4) % 8
        send("ak3", A.at[bb], A.at[bb], kk)

    fwd_a(0, 0)
    relay_a()
    fwd_z(1)
    spread_x(1)
    relay_x(0)
    mm1(0, 0)
    fwd_a(1, 0)
    act_relay()
    fwd_z(2)
    spread_x(2)
    fwd_a(0, 1)
    relay_x(1)
    mm1(1, 0)
    mm1(2, 0)
    fwd_a(2, 0)
    relayed_x(0)
    mm1(0, 1)
    stage2(0, 0)
    act_pass()
    fwd_z(3)
    spread_x(3)
    stage2(1, 0)
    stage2(2, 0)
    relay_x(2)
    fwd_a(1, 1)
    mm1(3, 0)
    mm1(4, 0)
    stage2(0, 1)
    relayed_x(1)
    mm1(1, 1)
    mm1(2, 1)
    act_far()
    fwd_a(3, 0)
    stage2(3, 0)
    stage2(4, 0)
    fwd_z(4)
    spread_x(4)
    l_a.wait()
    got("ak0", "ak1", "ak2", "ak3")
    mm2(0)
    relay_x(3)
    fwd_a(2, 1)
    rest_a(0)
    mm1(5, 0)
    mm1(6, 0)
    stage2(1, 1)
    stage2(2, 1)
    relayed_x(2)
    mm1(3, 1)
    mm1(4, 1)
    fwd_a(3, 1)
    stage2(5, 0)
    stage2(6, 0)
    stage3(0, 0)
    stage3(1, 0)
    stage3(2, 0)
    relay_x(4)
    fwd_a(4, 0)
    mm1(7, 0)
    stage3(0, 1)
    stage2(3, 1)
    stage2(4, 1)
    stage3(3, 0)
    stage3(4, 0)
    mm2(1)
    stage2(7, 0)
    stage3(1, 1)
    stage3(2, 1)
    relayed_x(3)
    rest_a(1)
    mm1(5, 1)
    mm1(6, 1)
    relayed_x(4)
    fwd_a(4, 1)
    mm1(7, 1)
    Mx[0] = jnp.broadcast_to(jnp.max(mx[...].astype(F32)), (8, 128))
    send("mk", Mx.at[0], Mx.at[1], kk)
    stage2(5, 1)
    stage2(6, 1)
    stage3(5, 0)
    stage3(6, 0)
    stage2(7, 1)
    got("mk")
    Mx[2] = jnp.maximum(Mx[0], Mx[1])
    send("m1", Mx.at[2], Mx.at[3], yp)
    send("m2", Mx.at[2], Mx.at[4], ym)
    send("m3", Mx.at[2], Mx.at[5], yy)
    stage3(3, 1)
    stage3(4, 1)
    stage3(7, 0)
    mm2(2)
    mm2(3)
    stage3(5, 1)
    stage3(6, 1)
    mm2(4)
    stage3(7, 1)
    mm2(5)
    mm2(6)
    mm2(7)
    got("m1", "m2", "m3")
    amax = jnp.maximum(jnp.maximum(Mx[2], Mx[3]), jnp.maximum(Mx[4], Mx[5]))
    gain = (peak_level / (amax + eps))[0:1, 0:1]
    factor = gain * scales[...]
    l_m.wait()
    for i in range(K // CH):
        r = pl.ds(i * CH, CH)
        acc[r, :] = mask_v[r, :].astype(F32) * factor * acc[r, :]
    for p in range(2):
        got(f"fmU{p}", f"fmL{p}", f"fpL{p}", f"fpU{p}")
        for i in range(2):
            r = pl.ds(i * HALF, HALF)
            total = pair_sum(0, p, r) + fin[0, p, r, :].astype(F32) + fin[1, p, r, :].astype(F32)
            din[xs[p] // 2, r, :] = total * gain
    for n in ev:
        if n[:3] != "sib":
            copy_of(n).wait_send()
    for s in range(8):
        b, mine, d = where(s)

        @pl.when(jnp.logical_not(mine))
        def _():
            for p in range(2):
                copy_of(f"sib{s}{p}").wait_send()


def on_device(activations, d_out, levels, scales, clip_mask):
    any_ = pl.BlockSpec(memory_space=pl.ANY)
    vm = pltpu.VMEM
    d_in_t, d_levels = pl.pallas_call(
        kernel,
        out_shape=(pltpu.VMEM((2, K, N), F32), pltpu.VMEM((K, C), F32)),
        in_specs=[any_, any_, any_, pl.BlockSpec(memory_space=vm), any_],
        out_specs=(pl.BlockSpec(memory_space=vm), pl.BlockSpec(memory_space=vm)),
        scratch_shapes=[
            vm((8, 4, 128, C), BF16),
            vm((8, K, T), BF16),
            vm((K, C), BF16),
            vm((4, 2, K, N), F32),
            vm((4, 2, K, N), BF16),
            vm((4, 2, K, N), BF16),
            vm((3, 2, K, N), BF16),
            vm((2, 2, HALF, N), BF16),
            vm((2, 2, K, N), BF16),
            vm((K, C), BF16),
            vm((K, C), jnp.int32),
            vm((16, C), BF16),
            vm((6, 8, 128), F32),
            pltpu.SemaphoreType.DMA((N_EV,)),
            pltpu.SemaphoreType.DMA((N_EV,)),
            pltpu.SemaphoreType.DMA((12,)),
        ],
        compiler_params=pltpu.CompilerParams(
            collective_id=0, has_side_effects=True, vmem_limit_bytes=50 * 2**20),
        cost_estimate=pl.CostEstimate(flops=4 * 4096 * K * C, bytes_accessed=12 * 2**20, transcendentals=0),
        name="fused",
    )(activations.T, d_out, levels, scales.reshape(1, C), clip_mask)
    return d_in_t.transpose(0, 2, 1).reshape(T, K), d_levels


def solution(mesh):
    placed = (P("col", "row"), P("row", "col"), P("row", "col"), P("col"), P("row", "col"))
    return jax.shard_map(
        on_device,
        mesh=mesh,
        in_specs=placed,
        out_specs=(P("col", "row"), P("row", "col")),
        check_vma=False,
    )
```

```python
import jax
import jax.numpy as jnp
from jax import lax
from jax.experimental import pallas as pl
from jax.experimental.pallas import tpu as pltpu
from jax.sharding import PartitionSpec as P

peak_level = 4.0
eps = 1e-06

MESH = pl.DeviceIdType.MESH
NT = (((1,), (1,)), ((), ()))
NN = (((1,), (0,)), ((), ()))
F32 = jnp.float32
BF16 = jnp.bfloat16

K = 832
T = 512
N = 256
C = 1024
XF = 48
HALF = K // 2
LO = pl.ds(0, HALF)
HI = pl.ds(HALF, HALF)
CH = 208
N_EV = 96

OFFS = (0, 1, 7, 2, 6, 3, 5, 4)


def up(h):
    return 2 * h - 1


def down(h):
    return 7 if h == 4 else 2 * h


def kernel(act, dout, levels, scales, mask, din, acc,
           D, A, W, Cs, Ssend, Srecv, Y, rel, fin, lev_v, mask_v, mx, Mx,
           ss, rs, ls):
    row, col = lax.axis_index("row"), lax.axis_index("col")
    z, x = row // 4, row % 4
    y, k = col // 2, col % 2

    def dev(dz=0, dx=0, dy=0, dk=0):
        return (((z + dz) % 8) * 4 + (x + dx) % 4, ((y + dy) % 4) * 2 + (k + dk) % 2)

    zp, zm, xp, xm = dev(dz=1), dev(dz=7), dev(dx=1), dev(dx=3)
    yp, ym, yy, kk = dev(dy=1), dev(dy=3), dev(dy=2), dev(dk=1)

    ev = {}

    def plan(name, src, dst, to):
        ev[name] = (len(ev), src, dst, to)

    def copy_of(name):
        i, src, dst, to = ev[name]
        return pltpu.make_async_remote_copy(
            src_ref=src, dst_ref=dst, send_sem=ss.at[i], recv_sem=rs.at[i],
            device_id=to, device_id_type=MESH)

    def send(name, *what):
        if what:
            plan(name, *what)
        copy_of(name).start()

    def got(*names):
        for n in names:
            copy_of(n).wait_recv()

    for p in range(2):
        plan(f"relL{p}", Y.at[2, p, LO], rel.at[0, p], yp)
        plan(f"relU{p}", Y.at[2, p, HI], rel.at[1, p], ym)
        plan(f"fmU{p}", Y.at[0, p, HI], fin.at[0, p, HI], yp)
        plan(f"fmL{p}", Y.at[0, p, LO], fin.at[0, p, LO], yp)
        plan(f"fpU{p}", Y.at[1, p, HI], fin.at[1, p, HI], ym)
        plan(f"fpL{p}", Y.at[1, p, LO], fin.at[1, p, LO], ym)
        for s in range(8):
            d = ((z + OFFS[s]) % 8 // 2 + 4 - y) % 4
            plan(f"sib{s}{p}", Ssend.at[d, p], Srecv.at[d, p], kk)
    xs = (x // 2 * 2, 2 - x // 2 * 2)

    own = 2 * y + k
    l_d = pltpu.make_async_copy(dout, D.at[0, x], ls.at[0])
    l_a = pltpu.make_async_copy(act, A.at[own], ls.at[1])
    l_w = pltpu.make_async_copy(levels, lev_v, ls.at[2])
    l_m = pltpu.make_async_copy(mask, mask_v, ls.at[3])

    barrier = pltpu.get_barrier_semaphore()
    peers = (zp, zm, xp, xm, yp, ym, yy, kk)
    for p in peers:
        pl.semaphore_signal(barrier, inc=1, device_id=p, device_id_type=MESH)
    l_d.start()
    l_w.start()
    l_a.start()
    pl.semaphore_wait(barrier, len(peers))

    a_rows, b_rows = pl.ds(0, XF), pl.ds(XF, 128 - XF)
    b_lo, b_hi = pl.ds(XF, 48), pl.ds(XF + 48, 80 - 48)

    send("xA+", dout.at[a_rows], D.at[0, x, a_rows], xp)
    send("xA-", dout.at[a_rows], D.at[0, x, a_rows], xm)
    send("zB+1", dout.at[b_rows], D.at[down(1), x, b_rows], zp)
    send("zB-1", dout.at[b_rows], D.at[up(1), x, b_rows], zm)
    l_m.start()
    mx[...] = jnp.zeros_like(mx)

    def start_x():
        send("xB+0", dout.at[b_rows], D.at[0, x, b_rows], xp)
        send("xB-0", dout.at[b_rows], D.at[0, x, b_rows], xm)

    def start_act1():
        send("aL+", act.at[LO], A.at[own, LO], yp)
        send("aU-", act.at[HI], A.at[own, HI], ym)

    def start_act2():
        send("aU+", act.at[HI], A.at[own, HI], yp)
        send("aL-", act.at[LO], A.at[own, LO], ym)

    def start_pair():
        send("ak0", act, A.at[own], kk)

    def deq():
        l_w.wait()

        def f(r):
            W[r, :] = (lev_v[r, :].astype(F32) * scales[...]).astype(BF16)
        rows_of(0, K, f)
        l_d.wait()

    def rows_of(lo, n, fn):
        def body(i, _):
            fn(pl.ds(pl.multiple_of(lo + i * CH, 16), CH))
            return 0
        lax.fori_loop(0, n // CH, body, 0)

    def fwd_z(h):
        got(f"zB+{h}", f"zB-{h}")
        if h < 3:
            send(f"zB+{h+1}", D.at[down(h), x, b_rows], D.at[down(h + 1), x, b_rows], zp)
            send(f"zB-{h+1}", D.at[up(h), x, b_rows], D.at[up(h + 1), x, b_rows], zm)
        if h == 3:
            send("zB+4", D.at[down(3), x, b_lo], D.at[7, x, b_lo], zp)
            send("zB-4", D.at[up(3), x, b_hi], D.at[7, x, b_hi], zm)

    def spread_x(h):
        pair = D.at[pl.ds(2 * h - 1, 2), x, b_rows] if h < 4 else D.at[7, x, b_rows]
        send(f"xB+{h}", pair, pair, xp)
        send(f"xB-{h}", pair, pair, xm)

    def fa(way, h, p):
        if h > 0:
            got(f"zA{p}{way}{h}")
        s = 0 if h == 0 else down(h) if way == "+" else up(h)
        to = down(h + 1) if way == "+" or h == 3 else up(h + 1)
        q = pl.ds(xs[p], 2)
        send(f"zA{p}{way}{h+1}", D.at[s, q, a_rows], D.at[to, q, a_rows], zp if way == "+" else zm)

    def ea(way, h, p):
        got(f"zA{p}{way}{h}")

    xl, xr = (x + 3) % 4, (x + 1) % 4

    def relay_a():
        got("xA+", "xA-")
        r0, r1 = D.at[0, xl, pl.ds(0, 32)], D.at[0, xr, pl.ds(32, 16)]
        send("xR+", r0, r0, xp)
        send("xR-", r1, r1, xm)

    def got_a():
        got("xR+", "xR-")

    def got_x(h):
        got(f"xB+{h}", f"xB-{h}")

    def relay_p(h):
        r = D.at[0 if h == 0 else 7, xl, b_lo] if h in (0, 4) else D.at[up(h), xl, b_rows]
        send(f"xr+{h}", r, r, xp)

    def relay_m(h):
        r = D.at[0 if h == 0 else 7, xr, b_hi] if h in (0, 4) else D.at[down(h), xr, b_rows]
        send(f"xr-{h}", r, r, xm)

    def got_p(h):
        got(f"xr+{h}")

    def got_m(h):
        got(f"xr-{h}")

    def where(s):
        b = (z + OFFS[s]) % 8
        return b, b % 2 == k, (b // 2 + 4 - y) % 4

    def mm1(s, p):
        b, mine, d = where(s)
        q = pl.ds(xs[p], 2)

        def part():
            return lax.dot_general(W[...], D[s, q].reshape(N, C), NT, preferred_element_type=F32)

        @pl.when(mine)
        def _():
            Cs[d, p] = part()

        @pl.when(jnp.logical_not(mine))
        def _():
            Ssend[d, p] = part().astype(BF16)
            send(f"sib{s}{p}")

        for j in range(2):
            def big(i, m):
                r = pl.multiple_of(i * 16, 16)
                return jnp.maximum(m, jnp.abs(D[s, xs[p] + j, pl.ds(r, 16), :]))

            mx[...] = lax.fori_loop(0, 8, big, mx[...], unroll=4)

    def pair_sum(d, p, r):
        return Cs[d, p, r, :] + Srecv[d, p, r, :].astype(F32)

    def stage2(s, p):
        b, mine, d = where(s)

        @pl.when(mine)
        def _():
            got(f"sib{s}{p}")

            @pl.when(d == 2)
            def _():
                def f(r):
                    Y[2, p, r, :] = pair_sum(2, p, r).astype(BF16)
                rows_of(0, K, f)
                send(f"relL{p}")
                send(f"relU{p}")

            @pl.when(d == 1)
            def _():
                def f(r):
                    Y[0, p, r, :] = pair_sum(1, p, r).astype(BF16)
                rows_of(HALF, HALF, f)
                send(f"fmU{p}")

            @pl.when(d == 3)
            def _():
                def f(r):
                    Y[1, p, r, :] = pair_sum(3, p, r).astype(BF16)
                rows_of(0, HALF, f)
                send(f"fpL{p}")

    def stage3(s, p):
        b, mine, d = where(s)

        @pl.when(jnp.logical_and(mine, d == 1))
        def _():
            got(f"relL{p}")

            def f(r):
                Y[0, p, r, :] = (pair_sum(1, p, r) + rel[0, p, r, :].astype(F32)).astype(BF16)
            rows_of(0, HALF, f)
            send(f"fmL{p}")

        @pl.when(jnp.logical_and(mine, d == 3))
        def _():
            got(f"relU{p}")

            def f(i, _):
                r = pl.ds(pl.multiple_of(HALF + i * CH, 16), CH)
                q = pl.ds(pl.multiple_of(i * CH, 16), CH)
                Y[1, p, r, :] = (pair_sum(3, p, r) + rel[1, p, q, :].astype(F32)).astype(BF16)
                return 0
            lax.fori_loop(0, HALF // CH, f, 0)
            send(f"fpU{p}")

    def block(s, j):
        return lax.dot_general(A[where(s)[0]], D.at[s][:, :, pl.ds(j * 256, 256)].reshape(T, 256),
                               NN, preferred_element_type=F32)

    def mm2(*slots):
        for j in range(C // 256):
            v = block(slots[0], j)
            for s in slots[1:]:
                v = v + block(s, j)
            c = pl.ds(j * 256, 256)
            if slots[0] == 0:
                acc[:, c] = v
            else:
                acc[:, c] += v

    def mm2_last():
        l_m.wait()
        factor = gain() * scales[...]
        for j in range(C // 256):
            c = pl.ds(j * 256, 256)
            acc[:, c] = (acc[:, c] + block(7, j)) * (mask_v[:, c].astype(F32) * factor[:, j * 256:(j + 1) * 256])

    def gain():
        amax = jnp.maximum(jnp.maximum(Mx[2], Mx[3]), jnp.maximum(Mx[4], Mx[5]))
        return (peak_level / (amax + eps))[0:1, 0:1]

    def peak_pair():
        Mx[0] = jnp.broadcast_to(jnp.max(mx[...].astype(F32)), (8, 128))
        send("mk", Mx.at[0], Mx.at[1], kk)

    def peak_col():
        got("mk")
        Mx[2] = jnp.maximum(Mx[0], Mx[1])
        send("m1", Mx.at[2], Mx.at[3], yp)
        send("m2", Mx.at[2], Mx.at[4], ym)
        send("m3", Mx.at[2], Mx.at[5], yy)

    def act_all():
        l_a.wait()
        got("ak0", "ak1", "ak2", "ak3")

    def finish(p):
        got(f"fmU{p}", f"fmL{p}", f"fpL{p}", f"fpU{p}")
        g = gain()

        def f(r):
            total = pair_sum(0, p, r) + fin[0, p, r, :].astype(F32) + fin[1, p, r, :].astype(F32)
            din[xs[p] // 2, r, :] = total * g
        rows_of(0, K, f)

    def act_relay():
        got("aL+", "aU-")
        bl, br = (own + 6) % 8, (own + 2) % 8
        send("aR+", A.at[bl, LO], A.at[bl, LO], yp)
        send("aR-", A.at[br, HI], A.at[br, HI], ym)

    def act_pass():
        got("aU+", "aL-")
        bl, br = (own + 6) % 8, (own + 2) % 8
        send("ak1", A.at[bl], A.at[bl], kk)
        send("ak2", A.at[br], A.at[br], kk)

    def act_far():
        got("aR+", "aR-")
        bb = (own + 4) % 8
        send("ak3", A.at[bb], A.at[bb], kk)

    start_act1()
    start_x()
    start_act2()
    deq()
    relay_a()
    fa("+", 0, 0)
    fa("-", 0, 0)
    start_pair()
    fwd_z(1)
    spread_x(1)
    fa("-", 1, 0)
    got_x(0)
    fa("+", 1, 0)
    fwd_z(2)
    spread_x(2)
    mm1(0, 0)
    got_x(1)
    mm1(1, 0)
    got_a()
    fa("+", 2, 0)
    fa("-", 2, 0)
    act_relay()
    mm1(2, 0)
    fwd_z(3)
    spread_x(3)
    got_x(2)
    fa("+", 0, 1)
    fa("-", 0, 1)
    mm1(4, 0)
    stage2(1, 0)
    act_pass()
    fwd_z(4)
    stage2(4, 0)
    spread_x(4)
    mm1(3, 0)
    relay_m(0)
    stage2(0, 0)
    act_far()
    relay_p(0)
    fa("+", 3, 0)
    got_x(3)
    ea("-", 3, 0)
    relay_p(1)
    relay_m(1)
    fa("-", 1, 1)
    mm1(5, 0)
    relay_p(2)
    stage2(3, 0)
    mm1(6, 0)
    relay_p(3)
    stage2(2, 0)
    act_all()
    fa("+", 1, 1)
    ea("+", 4, 0)
    got_m(0)
    got_x(4)
    stage2(6, 0)
    relay_m(2)
    stage2(5, 0)
    relay_m(3)
    got_p(0)
    mm1(7, 0)
    relay_m(4)
    mm1(0, 1)
    stage3(2, 0)
    fa("-", 2, 1)
    relay_p(4)
    fa("+", 2, 1)
    got_m(1)
    got_p(1)
    mm1(2, 1)
    stage2(7, 0)
    mm2(0)
    mm1(1, 1)
    got_p(2)
    stage3(1, 0)
    fa("-", 3, 1)
    mm1(3, 1)
    stage3(4, 0)
    got_m(2)
    stage3(3, 0)
    stage2(0, 1)
    mm1(4, 1)
    got_m(3)
    stage2(2, 1)
    stage2(1, 1)
    stage3(0, 0)
    stage3(5, 0)
    got_p(3)
    ea("+", 3, 1)
    stage3(7, 0)
    mm1(5, 1)
    mm1(6, 1)
    stage2(3, 1)
    got_m(4)
    stage3(6, 0)
    stage2(4, 1)
    got_p(4)
    ea("-", 4, 1)
    mm1(7, 1)
    stage2(6, 1)
    peak_pair()
    mm2(5, 6)
    stage2(5, 1)
    stage2(7, 1)
    stage3(2, 1)
    mm2(3, 4)
    peak_col()
    stage3(0, 1)
    stage3(1, 1)
    stage3(3, 1)
    stage3(4, 1)
    mm2(1, 2)
    stage3(7, 1)
    stage3(6, 1)
    got("m1", "m2", "m3")
    finish(0)
    stage3(5, 1)
    mm2_last()
    finish(1)
    for n in ev:
        if n[:3] != "sib":
            copy_of(n).wait_send()
    for s in range(8):
        b, mine, d = where(s)

        @pl.when(jnp.logical_not(mine))
        def _():
            for p in range(2):
                copy_of(f"sib{s}{p}").wait_send()


def store(din, dlev, din_out, dlev_out, sems):
    copies = [pltpu.make_async_copy(din.at[p], din_out.at[:, pl.ds(p * N, N)], sems.at[p]) for p in range(2)]
    for i in range(4):
        r = pl.ds(i * CH, CH)
        copies.append(pltpu.make_async_copy(dlev.at[r], dlev_out.at[r], sems.at[2 + i]))
    for c in copies:
        c.start()
    for c in copies:
        c.wait()


def on_device(activations, d_out, levels, scales, clip_mask):
    any_ = pl.BlockSpec(memory_space=pl.ANY)
    vm = pltpu.VMEM
    d_in_t, d_levels = pl.pallas_call(
        kernel,
        out_shape=(pltpu.VMEM((2, K, N), F32), pltpu.VMEM((K, C), F32)),
        in_specs=[any_, any_, any_, pl.BlockSpec(memory_space=vm), any_],
        out_specs=(pl.BlockSpec(memory_space=vm), pl.BlockSpec(memory_space=vm)),
        scratch_shapes=[
            vm((8, 4, 128, C), BF16),
            vm((8, K, T), BF16),
            vm((K, C), BF16),
            vm((4, 2, K, N), F32),
            vm((4, 2, K, N), BF16),
            vm((4, 2, K, N), BF16),
            vm((3, 2, K, N), BF16),
            vm((2, 2, HALF, N), BF16),
            vm((2, 2, K, N), BF16),
            vm((K, C), BF16),
            vm((K, C), jnp.int32),
            vm((16, C), BF16),
            vm((6, 8, 128), F32),
            pltpu.SemaphoreType.DMA((N_EV,)),
            pltpu.SemaphoreType.DMA((N_EV,)),
            pltpu.SemaphoreType.DMA((12,)),
        ],
        compiler_params=pltpu.CompilerParams(
            collective_id=0, has_side_effects=True, vmem_limit_bytes=50 * 2**20),
        cost_estimate=pl.CostEstimate(flops=4 * 4096 * K * C, bytes_accessed=12 * 2**20, transcendentals=0),
        name="fused",
    )(activations.T, d_out, levels, scales.reshape(1, C), clip_mask)
    d_in_t = pltpu.with_memory_space_constraint(d_in_t, vm)
    d_levels = pltpu.with_memory_space_constraint(d_levels, vm)
    d_in_t, d_levels = pl.pallas_call(
        store,
        out_shape=(jax.ShapeDtypeStruct((K, T), F32), jax.ShapeDtypeStruct((K, C), F32)),
        in_specs=[pl.BlockSpec(memory_space=vm)] * 2,
        out_specs=(any_, any_),
        scratch_shapes=[pltpu.SemaphoreType.DMA((6,))],
        compiler_params=pltpu.CompilerParams(vmem_limit_bytes=8 * 2**20),
        name="store",
    )(d_in_t, d_levels)
    return d_in_t.T, d_levels


def solution(mesh):
    placed = (P("col", "row"), P("row", "col"), P("row", "col"), P("col"), P("row", "col"))
    return jax.shard_map(
        on_device,
        mesh=mesh,
        in_specs=placed,
        out_specs=(P("col", "row"), P("row", "col")),
        check_vma=False,
    )
```

```python
import jax
import jax.numpy as jnp
from jax import lax
from jax.experimental import pallas as pl
from jax.experimental.pallas import tpu as pltpu
from jax.sharding import PartitionSpec as P

peak_level = 4.0
eps = 1e-06

MESH = pl.DeviceIdType.MESH
NT = (((1,), (1,)), ((), ()))
NN = (((1,), (0,)), ((), ()))
F32 = jnp.float32
BF16 = jnp.bfloat16

K = 832
T = 512
N = 256
C = 1024
XF = 48
HALF = K // 2
LO = pl.ds(0, HALF)
HI = pl.ds(HALF, HALF)
CH = 208
N_EV = 96

OFFS = (0, 1, 7, 2, 6, 3, 5, 4)


def up(h):
    return 2 * h - 1


def down(h):
    return 7 if h == 4 else 2 * h


def kernel(act, dout, levels, scales, mask, din, acc,
           D, A, W, Cs, Ssend, Srecv, Y, rel, fin, lev_v, mask_v, mx, Mx,
           ss, rs, ls):
    row, col = lax.axis_index("row"), lax.axis_index("col")
    z, x = row // 4, row % 4
    y, k = col // 2, col % 2

    def dev(dz=0, dx=0, dy=0, dk=0):
        return (((z + dz) % 8) * 4 + (x + dx) % 4, ((y + dy) % 4) * 2 + (k + dk) % 2)

    zp, zm, xp, xm = dev(dz=1), dev(dz=7), dev(dx=1), dev(dx=3)
    yp, ym, yy, kk = dev(dy=1), dev(dy=3), dev(dy=2), dev(dk=1)

    ev = {}

    def plan(name, src, dst, to):
        ev[name] = (len(ev), src, dst, to)

    def copy_of(name):
        i, src, dst, to = ev[name]
        return pltpu.make_async_remote_copy(
            src_ref=src, dst_ref=dst, send_sem=ss.at[i], recv_sem=rs.at[i],
            device_id=to, device_id_type=MESH)

    def send(name, *what):
        if what:
            plan(name, *what)
        copy_of(name).start()

    def got(*names):
        for n in names:
            copy_of(n).wait_recv()

    for p in range(2):
        plan(f"relL{p}", Y.at[2, p, LO], rel.at[0, p], yp)
        plan(f"relU{p}", Y.at[2, p, HI], rel.at[1, p], ym)
        plan(f"fmU{p}", Y.at[0, p, HI], fin.at[0, p, HI], yp)
        plan(f"fmL{p}", Y.at[0, p, LO], fin.at[0, p, LO], yp)
        plan(f"fpU{p}", Y.at[1, p, HI], fin.at[1, p, HI], ym)
        plan(f"fpL{p}", Y.at[1, p, LO], fin.at[1, p, LO], ym)
        for s in range(8):
            d = ((z + OFFS[s]) % 8 // 2 + 4 - y) % 4
            plan(f"sib{s}{p}", Ssend.at[d, p], Srecv.at[d, p], kk)
    xs = (x // 2 * 2, 2 - x // 2 * 2)

    own = 2 * y + k
    l_d = pltpu.make_async_copy(dout, D.at[0, x], ls.at[0])
    l_a = pltpu.make_async_copy(act, A.at[own], ls.at[1])
    l_w = pltpu.make_async_copy(levels, lev_v, ls.at[2])
    l_m = pltpu.make_async_copy(mask, mask_v, ls.at[3])

    barrier = pltpu.get_barrier_semaphore()
    peers = (zp, zm, xp, xm, yp, ym, yy, kk)
    for p in peers:
        pl.semaphore_signal(barrier, inc=1, device_id=p, device_id_type=MESH)
    l_d.start()
    l_w.start()
    l_a.start()
    pl.semaphore_wait(barrier, len(peers))

    a_rows, b_rows = pl.ds(0, XF), pl.ds(XF, 128 - XF)
    b_lo, b_hi = pl.ds(XF, 48), pl.ds(XF + 48, 80 - 48)

    send("xA+", dout.at[a_rows], D.at[0, x, a_rows], xp)
    send("xA-", dout.at[a_rows], D.at[0, x, a_rows], xm)
    send("zB+1", dout.at[b_rows], D.at[down(1), x, b_rows], zp)
    send("zB-1", dout.at[b_rows], D.at[up(1), x, b_rows], zm)
    l_m.start()
    mx[...] = jnp.zeros_like(mx)

    def start_x():
        send("xB+0", dout.at[b_rows], D.at[0, x, b_rows], xp)
        send("xB-0", dout.at[b_rows], D.at[0, x, b_rows], xm)

    def start_act1():
        send("aL+", act.at[LO], A.at[own, LO], yp)
        send("aU-", act.at[HI], A.at[own, HI], ym)

    def start_act2():
        send("aU+", act.at[HI], A.at[own, HI], yp)
        send("aL-", act.at[LO], A.at[own, LO], ym)

    def start_pair():
        send("ak0", act, A.at[own], kk)

    def deq():
        l_w.wait()

        def f(r):
            W[r, :] = (lev_v[r, :].astype(F32) * scales[...]).astype(BF16)
        rows_of(0, K, f)
        l_d.wait()

    def rows_of(lo, n, fn):
        def body(i, _):
            fn(pl.ds(pl.multiple_of(lo + i * CH, 16), CH))
            return 0
        lax.fori_loop(0, n // CH, body, 0)

    def fwd_z(h):
        got(f"zB+{h}", f"zB-{h}")
        if h < 3:
            send(f"zB+{h+1}", D.at[down(h), x, b_rows], D.at[down(h + 1), x, b_rows], zp)
            send(f"zB-{h+1}", D.at[up(h), x, b_rows], D.at[up(h + 1), x, b_rows], zm)
        if h == 3:
            send("zB+4", D.at[down(3), x, b_lo], D.at[7, x, b_lo], zp)
            send("zB-4", D.at[up(3), x, b_hi], D.at[7, x, b_hi], zm)

    def spread_x(h):
        pair = D.at[pl.ds(2 * h - 1, 2), x, b_rows] if h < 4 else D.at[7, x, b_rows]
        send(f"xB+{h}", pair, pair, xp)
        send(f"xB-{h}", pair, pair, xm)

    def fa(way, h, p):
        if h > 0:
            got(f"zA{p}{way}{h}")
        s = 0 if h == 0 else down(h) if way == "+" else up(h)
        to = down(h + 1) if way == "+" or h == 3 else up(h + 1)
        q = pl.ds(xs[p], 2)
        send(f"zA{p}{way}{h+1}", D.at[s, q, a_rows], D.at[to, q, a_rows], zp if way == "+" else zm)

    def ea(way, h, p):
        got(f"zA{p}{way}{h}")

    xl, xr = (x + 3) % 4, (x + 1) % 4

    def relay_a():
        got("xA+", "xA-")
        r0, r1 = D.at[0, xl, pl.ds(0, 32)], D.at[0, xr, pl.ds(32, 16)]
        send("xR+", r0, r0, xp)
        send("xR-", r1, r1, xm)

    def got_a():
        got("xR+", "xR-")

    def got_x(h):
        got(f"xB+{h}", f"xB-{h}")

    def relay_p(h):
        r = D.at[0 if h == 0 else 7, xl, b_lo] if h in (0, 4) else D.at[up(h), xl, b_rows]
        send(f"xr+{h}", r, r, xp)

    def relay_m(h):
        r = D.at[0 if h == 0 else 7, xr, b_hi] if h in (0, 4) else D.at[down(h), xr, b_rows]
        send(f"xr-{h}", r, r, xm)

    def got_p(h):
        got(f"xr+{h}")

    def got_m(h):
        got(f"xr-{h}")

    def where(s):
        b = (z + OFFS[s]) % 8
        return b, b % 2 == k, (b // 2 + 4 - y) % 4

    def mm1(s, p):
        b, mine, d = where(s)
        q = pl.ds(xs[p], 2)

        def part():
            return lax.dot_general(W[...], D[s, q].reshape(N, C), NT, preferred_element_type=F32)

        @pl.when(mine)
        def _():
            Cs[d, p] = part()

        @pl.when(jnp.logical_not(mine))
        def _():
            Ssend[d, p] = part().astype(BF16)
            send(f"sib{s}{p}")

        for j in range(2):
            def big(i, m):
                r = pl.multiple_of(i * 16, 16)
                return jnp.maximum(m, jnp.abs(D[s, xs[p] + j, pl.ds(r, 16), :]))

            mx[...] = lax.fori_loop(0, 8, big, mx[...], unroll=4)

    def pair_sum(d, p, r):
        return Cs[d, p, r, :] + Srecv[d, p, r, :].astype(F32)

    def stage2(s, p):
        b, mine, d = where(s)

        @pl.when(mine)
        def _():
            got(f"sib{s}{p}")

            @pl.when(d == 2)
            def _():
                def f(r):
                    Y[2, p, r, :] = pair_sum(2, p, r).astype(BF16)
                rows_of(0, K, f)
                send(f"relL{p}")
                send(f"relU{p}")

            @pl.when(d == 1)
            def _():
                def f(r):
                    Y[0, p, r, :] = pair_sum(1, p, r).astype(BF16)
                rows_of(HALF, HALF, f)
                send(f"fmU{p}")

            @pl.when(d == 3)
            def _():
                def f(r):
                    Y[1, p, r, :] = pair_sum(3, p, r).astype(BF16)
                rows_of(0, HALF, f)
                send(f"fpL{p}")

    def stage3(s, p):
        b, mine, d = where(s)

        @pl.when(jnp.logical_and(mine, d == 1))
        def _():
            got(f"relL{p}")

            def f(r):
                Y[0, p, r, :] = (pair_sum(1, p, r) + rel[0, p, r, :].astype(F32)).astype(BF16)
            rows_of(0, HALF, f)
            send(f"fmL{p}")

        @pl.when(jnp.logical_and(mine, d == 3))
        def _():
            got(f"relU{p}")

            def f(i, _):
                r = pl.ds(pl.multiple_of(HALF + i * CH, 16), CH)
                q = pl.ds(pl.multiple_of(i * CH, 16), CH)
                Y[1, p, r, :] = (pair_sum(3, p, r) + rel[1, p, q, :].astype(F32)).astype(BF16)
                return 0
            lax.fori_loop(0, HALF // CH, f, 0)
            send(f"fpU{p}")

    def block(s, j):
        return lax.dot_general(A[where(s)[0]], D.at[s][:, :, pl.ds(j * 256, 256)].reshape(T, 256),
                               NN, preferred_element_type=F32)

    def mm2(*slots):
        for j in range(C // 256):
            v = block(slots[0], j)
            for s in slots[1:]:
                v = v + block(s, j)
            c = pl.ds(j * 256, 256)
            if slots[0] == 0:
                acc[:, c] = v
            else:
                acc[:, c] += v

    def mm2_last():
        l_m.wait()
        factor = gain() * scales[...]
        for j in range(C // 256):
            c = pl.ds(j * 256, 256)
            acc[:, c] = (acc[:, c] + block(7, j)) * (mask_v[:, c].astype(F32) * factor[:, j * 256:(j + 1) * 256])

    def gain():
        amax = jnp.maximum(jnp.maximum(Mx[2], Mx[3]), jnp.maximum(Mx[4], Mx[5]))
        return (peak_level / (amax + eps))[0:1, 0:1]

    def peak_pair():
        Mx[0] = jnp.broadcast_to(jnp.max(mx[...].astype(F32)), (8, 128))
        send("mk", Mx.at[0], Mx.at[1], kk)

    def peak_col():
        got("mk")
        Mx[2] = jnp.maximum(Mx[0], Mx[1])
        send("m1", Mx.at[2], Mx.at[3], yp)
        send("m2", Mx.at[2], Mx.at[4], ym)
        send("m3", Mx.at[2], Mx.at[5], yy)

    def act_all():
        l_a.wait()
        got("ak0", "ak1", "ak2", "ak3")

    def finish(p):
        got(f"fmU{p}", f"fmL{p}", f"fpL{p}", f"fpU{p}")
        g = gain()

        def f(r):
            total = pair_sum(0, p, r) + fin[0, p, r, :].astype(F32) + fin[1, p, r, :].astype(F32)
            din[xs[p] // 2, r, :] = total * g
        rows_of(0, K, f)

    def act_relay():
        got("aL+", "aU-")
        bl, br = (own + 6) % 8, (own + 2) % 8
        send("aR+", A.at[bl, LO], A.at[bl, LO], yp)
        send("aR-", A.at[br, HI], A.at[br, HI], ym)

    def act_pass():
        got("aU+", "aL-")
        bl, br = (own + 6) % 8, (own + 2) % 8
        send("ak1", A.at[bl], A.at[bl], kk)
        send("ak2", A.at[br], A.at[br], kk)

    def act_far():
        got("aR+", "aR-")
        bb = (own + 4) % 8
        send("ak3", A.at[bb], A.at[bb], kk)

    start_act1()
    start_x()
    start_act2()
    deq()
    relay_a()
    fa("+", 0, 0)
    fa("-", 0, 0)
    start_pair()
    fwd_z(1)
    spread_x(1)
    fa("-", 1, 0)
    got_x(0)
    fa("+", 1, 0)
    fwd_z(2)
    spread_x(2)
    mm1(0, 0)
    got_x(1)
    mm1(1, 0)
    got_a()
    fa("+", 2, 0)
    fa("-", 2, 0)
    act_relay()
    mm1(2, 0)
    fwd_z(3)
    spread_x(3)
    got_x(2)
    fa("+", 0, 1)
    fa("-", 0, 1)
    mm1(4, 0)
    stage2(1, 0)
    act_pass()
    fwd_z(4)
    stage2(4, 0)
    spread_x(4)
    mm1(3, 0)
    relay_m(0)
    stage2(0, 0)
    act_far()
    relay_p(0)
    fa("+", 3, 0)
    got_x(3)
    ea("-", 3, 0)
    relay_p(1)
    relay_m(1)
    fa("-", 1, 1)
    mm1(5, 0)
    relay_p(2)
    stage2(3, 0)
    mm1(6, 0)
    relay_p(3)
    stage2(2, 0)
    act_all()
    fa("+", 1, 1)
    ea("+", 4, 0)
    got_m(0)
    got_x(4)
    stage2(6, 0)
    relay_m(2)
    stage2(5, 0)
    relay_m(3)
    got_p(0)
    mm1(7, 0)
    relay_m(4)
    mm1(0, 1)
    stage3(2, 0)
    fa("-", 2, 1)
    relay_p(4)
    fa("+", 2, 1)
    got_m(1)
    got_p(1)
    mm1(2, 1)
    stage2(7, 0)
    mm2(0)
    mm1(1, 1)
    got_p(2)
    stage3(1, 0)
    fa("-", 3, 1)
    mm1(3, 1)
    stage3(4, 0)
    got_m(2)
    stage3(3, 0)
    stage2(0, 1)
    mm1(4, 1)
    got_m(3)
    stage2(2, 1)
    stage2(1, 1)
    stage3(0, 0)
    stage3(5, 0)
    got_p(3)
    ea("+", 3, 1)
    stage3(7, 0)
    mm1(5, 1)
    mm1(6, 1)
    stage2(3, 1)
    got_m(4)
    stage3(6, 0)
    stage2(4, 1)
    got_p(4)
    ea("-", 4, 1)
    mm1(7, 1)
    stage2(5, 1)
    stage2(6, 1)
    peak_pair()
    mm2(5, 6)
    stage2(7, 1)
    stage3(2, 1)
    mm2(3, 4)
    peak_col()
    stage3(0, 1)
    stage3(1, 1)
    stage3(3, 1)
    stage3(4, 1)
    mm2(1, 2)
    stage3(5, 1)
    stage3(6, 1)
    stage3(7, 1)
    got("m1", "m2", "m3")
    finish(0)
    mm2_last()
    finish(1)
    for n in ev:
        if n[:3] != "sib":
            copy_of(n).wait_send()
    for s in range(8):
        b, mine, d = where(s)

        @pl.when(jnp.logical_not(mine))
        def _():
            for p in range(2):
                copy_of(f"sib{s}{p}").wait_send()


def store(din, dlev, din_out, dlev_out, sems):
    copies = [pltpu.make_async_copy(din.at[p], din_out.at[:, pl.ds(p * N, N)], sems.at[p]) for p in range(2)]
    for i in range(4):
        r = pl.ds(i * CH, CH)
        copies.append(pltpu.make_async_copy(dlev.at[r], dlev_out.at[r], sems.at[2 + i]))
    for c in copies:
        c.start()
    for c in copies:
        c.wait()


def on_device(activations, d_out, levels, scales, clip_mask):
    any_ = pl.BlockSpec(memory_space=pl.ANY)
    vm = pltpu.VMEM
    d_in_t, d_levels = pl.pallas_call(
        kernel,
        out_shape=(pltpu.VMEM((2, K, N), F32), pltpu.VMEM((K, C), F32)),
        in_specs=[any_, any_, any_, pl.BlockSpec(memory_space=vm), any_],
        out_specs=(pl.BlockSpec(memory_space=vm), pl.BlockSpec(memory_space=vm)),
        scratch_shapes=[
            vm((8, 4, 128, C), BF16),
            vm((8, K, T), BF16),
            vm((K, C), BF16),
            vm((4, 2, K, N), F32),
            vm((4, 2, K, N), BF16),
            vm((4, 2, K, N), BF16),
            vm((3, 2, K, N), BF16),
            vm((2, 2, HALF, N), BF16),
            vm((2, 2, K, N), BF16),
            vm((K, C), BF16),
            vm((K, C), jnp.int32),
            vm((16, C), BF16),
            vm((6, 8, 128), F32),
            pltpu.SemaphoreType.DMA((N_EV,)),
            pltpu.SemaphoreType.DMA((N_EV,)),
            pltpu.SemaphoreType.DMA((12,)),
        ],
        compiler_params=pltpu.CompilerParams(
            collective_id=0, has_side_effects=True, vmem_limit_bytes=50 * 2**20),
        cost_estimate=pl.CostEstimate(flops=4 * 4096 * K * C, bytes_accessed=12 * 2**20, transcendentals=0),
        name="fused",
    )(activations.T, d_out, levels, scales.reshape(1, C), clip_mask)
    d_in_t = pltpu.with_memory_space_constraint(d_in_t, vm)
    d_levels = pltpu.with_memory_space_constraint(d_levels, vm)
    d_in_t, d_levels = pl.pallas_call(
        store,
        out_shape=(jax.ShapeDtypeStruct((K, T), F32), jax.ShapeDtypeStruct((K, C), F32)),
        in_specs=[pl.BlockSpec(memory_space=vm)] * 2,
        out_specs=(any_, any_),
        scratch_shapes=[pltpu.SemaphoreType.DMA((6,))],
        compiler_params=pltpu.CompilerParams(vmem_limit_bytes=8 * 2**20),
        name="store",
    )(d_in_t, d_levels)
    return d_in_t.T, d_levels


def solution(mesh):
    placed = (P("col", "row"), P("row", "col"), P("row", "col"), P("col"), P("row", "col"))
    return jax.shard_map(
        on_device,
        mesh=mesh,
        in_specs=placed,
        out_specs=(P("col", "row"), P("row", "col")),
        check_vma=False,
    )
```
